512 devices in a mesh: pipe: 4 (over y_hi), tensor: 32 (over x, z), dp: 4 (over y_lo, core).
Axes of the slice: x: 4, y: 8 (y_hi: 4, y_lo: 2; y = y_hi * 2 + y_lo), z: 8, core: 2. Of those that a mesh axis runs over, the one named last changes fastest.
Arguments:
- section_input: bfloat16 [4, 1, 4, 128, 6144], P('pipe', None, 'dp', 'tensor'), may hold values from -6 to 6
- pre_act: bfloat16 [4, 1, 4, 128, 8192], P('pipe', None, 'dp', None, 'tensor'), may hold values from -8 to 8
- cotangent: bfloat16 [1, 4, 128, 6144], P(None, 'dp', 'tensor'), may hold values from -6 to 6
- w_up: bfloat16 [4, 6144, 8192], P('pipe', 'dp', 'tensor'), may hold values from -0.078125 to 0.078125
- w_down: bfloat16 [4, 8192, 6144], P('pipe', 'tensor', 'dp'), may hold values from -0.0625 to 0.0625
Outputs:
- input_grad: bfloat16 [4, 1, 4, 128, 6144], P('pipe', None, 'dp', 'tensor')
- up_grad: bfloat16 [4, 6144, 8192], P('pipe', 'dp', 'tensor')
- down_grad: bfloat16 [4, 8192, 6144], P('pipe', 'tensor', 'dp')
The draws below stay inside these ranges and needn't reach their ends.
All inputs are finite; a program needn't handle non-finite values.
Results may differ from the reference program's by a relative error of at most 0.034.
Values may be sent and summed in bfloat16 or wider, within the bound.
No kernel may reach another device: no remote copies, remote signals or barrier semaphores. Data moves between devices by JAX's collectives and lax.ppermute only.
A program may use at most 64 MiB of HBM per device.

```python
import jax
import jax.numpy as jnp
from jax import lax

D = 6144
FF = 8192
ROWS = 128
MB = 1
SECTIONS = 4
GROUPS = 4
N_TENSOR = 32


def steps_of(stream_key, dims, cuts, least, largest):
    def one(dim, shards_of):
        heights = jax.random.uniform(jax.random.fold_in(jax.random.fold_in(stream_key, 6), dim), (shards_of,), jnp.float32, least / len(cuts), largest / len(cuts))
        return jnp.repeat(jnp.exp(heights), dims[dim] // shards_of).reshape((-1,) + (1,) * (len(dims) - dim - 1))

    gain = one(*cuts[0])
    for cut in cuts[1:]:
        gain = gain * one(*cut)
    return gain


def centred(stream_key, dims, width, limit, cuts=(), kind=jnp.bfloat16):
    result = width * jax.random.normal(stream_key, dims, jnp.float32)
    if cuts:
        result = result * steps_of(stream_key, dims, cuts, -0.22, 0.18)
    return jnp.clip(result, -limit, limit).astype(kind)


def setup_inputs(seed: int = 0) -> dict:
    arg_keys = jax.random.split(jax.random.key(seed), 6)
    return {
        "section_input": centred(arg_keys[0], (SECTIONS, MB, GROUPS, ROWS, D), 1.0, 6.0, ((0, 4), (2, 4), (3, 32))),
        "pre_act": centred(arg_keys[1], (SECTIONS, MB, GROUPS, ROWS, FF), 1.5, 8.0, ((0, 4), (2, 4), (4, 32))),
        "cotangent": centred(arg_keys[2], (MB, GROUPS, ROWS, D), 1.0, 6.0, ((1, 4), (2, 32))),
        "w_up": centred(arg_keys[3], (SECTIONS, D, FF), D ** -0.5, 0.078125, ((0, 4), (1, 4), (2, 32))),
        "w_down": centred(arg_keys[4], (SECTIONS, FF, D), FF ** -0.5, 0.0625, ((0, 4), (1, 32), (2, 4))),
    }


epsilon = 1e-06

def reference(section_input, pre_act, cotangent, w_up, w_down):
    section_count = section_input.shape[0]
    micro_count = section_input.shape[1]
    token_count = GROUPS * ROWS
    block_width = FF // N_TENSOR
    incoming = cotangent.reshape(micro_count, token_count, D)
    input_list = []
    up_list = []
    down_list = []
    for section in reversed(range(section_count)):
        inputs = section_input[section].reshape(micro_count, token_count, D).astype(jnp.float32)
        preact = pre_act[section].reshape(micro_count, token_count, FF).astype(jnp.float32)
        inverse = lax.rsqrt(lax.optimization_barrier(jnp.mean(inputs * inputs, axis=-1, keepdims=True)) + epsilon)
        normed = (inputs * inverse).astype(jnp.bfloat16)
        sigmoid_u = jax.nn.sigmoid(preact)
        hidden = (preact * sigmoid_u).astype(jnp.bfloat16)
        slope = sigmoid_u * (1.0 + preact * (1.0 - sigmoid_u))
        incoming_f = incoming.astype(jnp.float32)
        hidden_grad = jnp.einsum('mtd,fd->mtf', incoming_f, w_down[section].astype(jnp.float32))
        pre_grad = (hidden_grad * slope).astype(jnp.bfloat16)
        normed_grad = jnp.zeros((micro_count, token_count, D), jnp.float32)
        for part_index in range(N_TENSOR):
            lower = part_index * block_width
            piece = pre_grad[:, :, lower:lower + block_width].astype(jnp.float32)
            weight_piece = w_up[section][:, lower:lower + block_width].astype(jnp.float32)
            partial_sum = jnp.einsum('mtf,df->mtd', piece, weight_piece).astype(jnp.bfloat16)
            partial_sum = lax.optimization_barrier(partial_sum)
            normed_grad = normed_grad + partial_sum.astype(jnp.float32)
        mean_term = lax.optimization_barrier(jnp.mean(normed_grad * inputs, axis=-1, keepdims=True))
        grad_f = incoming_f + inverse * normed_grad - inputs * inverse ** 3 * mean_term
        outgoing = grad_f.astype(jnp.bfloat16)
        down_list.append(jnp.einsum('mtf,mtd->fd', hidden.astype(jnp.float32), incoming_f).astype(jnp.bfloat16))
        up_list.append(jnp.einsum('mtd,mtf->df', normed.astype(jnp.float32), pre_grad.astype(jnp.float32)).astype(jnp.bfloat16))
        input_list.append(outgoing.reshape(micro_count, GROUPS, ROWS, D))
        incoming = outgoing
    input_grad = jnp.stack(input_list[::-1])
    up_grad = jnp.stack(up_list[::-1])
    down_grad = jnp.stack(down_list[::-1])
    return (input_grad, up_grad, down_grad)
```

```python
import jax
import jax.numpy as jnp
from jax import lax
from jax.sharding import PartitionSpec as P

epsilon = 1e-06
f32 = jnp.float32
bf16 = jnp.bfloat16
LANES = 128


def exchange(blocks, axis):
    shape = blocks.shape
    flat = blocks.reshape(shape[0], -1, LANES)
    return lax.all_to_all(flat, axis, 0, 0).reshape(shape)


def after(value, *others):
    return lax.optimization_barrier((value,) + others)[0]


def per_device(section_input, pre_act, cotangent, w_up, w_down):
    pipe = lax.axis_size("pipe")
    parts = lax.axis_size("tensor")
    groups = lax.axis_size("dp")
    pipe_index = lax.axis_index("pipe")
    own_rows, width = section_input.shape[-2:]
    block = width // groups
    rows, hidden_width = pre_act.shape[-2:]
    tokens = parts * groups

    x_own = section_input[0, 0, 0]
    u_own = pre_act[0, 0, 0]
    x_own_f = x_own.astype(f32)
    inverse_own = lax.rsqrt(jnp.mean(x_own_f * x_own_f, axis=-1, keepdims=True) + epsilon)
    normed_own = (x_own_f * inverse_own).astype(bf16)

    down_all = lax.all_gather(w_down[0], "pipe", axis=0)
    up_all = lax.all_gather(w_up[0], "pipe", axis=0)

    cot_row = lax.dynamic_index_in_dim(cotangent[0, 0], pipe_index, 0, keepdims=False)
    grad = exchange(cot_row.reshape(groups, block), "dp")

    x_blocks = exchange(x_own.reshape(pipe * groups, block), ("pipe", "dp"))
    x_blocks = x_blocks.reshape(pipe, groups, block).astype(f32)
    square = lax.psum(jnp.sum(x_blocks * x_blocks, axis=-1), "dp")
    inverse = lax.rsqrt(square / width + epsilon)[..., None]

    u_rows = jnp.swapaxes(u_own.reshape(parts, pipe, hidden_width), 0, 1)
    u_rows = exchange(u_rows, "pipe")
    u_rows = lax.all_gather(u_rows, "dp", axis=2)
    u_rows = u_rows.reshape(pipe, tokens, hidden_width).astype(f32)
    sigmoid_u = jax.nn.sigmoid(u_rows)
    slope = sigmoid_u * (1.0 + u_rows * (1.0 - sigmoid_u))

    u_f = u_own.astype(f32)
    hidden = (u_f * jax.nn.sigmoid(u_f)).astype(bf16)
    hidden_all = lax.all_gather(hidden, "dp", axis=0)

    normed_blocks = exchange(
        jnp.swapaxes(normed_own.reshape(own_rows, groups, block), 0, 1), "dp"
    )
    normed_blocks = after(normed_blocks, up_all, down_all)
    normed_all = lax.all_gather(normed_blocks, "tensor", axis=0)

    rows_store, pre_store, out_store = [], [], []
    for section in reversed(range(pipe)):
        spread = jnp.broadcast_to(grad[None], (parts,) + grad.shape)
        grad_rows = exchange(spread, "tensor").reshape(tokens, block)
        rows_store.append(grad_rows)
        partial = lax.dot_general(
            grad_rows, down_all[section], (((1,), (1,)), ((), ())), preferred_element_type=f32
        ).astype(bf16)
        partials = lax.all_gather(partial, "dp", axis=0)
        hidden_grad = jnp.sum(partials.astype(f32), axis=0)
        pre_grad = (hidden_grad * slope[section]).astype(bf16)
        pre_store.append(pre_grad)
        pieces = lax.dot_general(
            pre_grad, up_all[section], (((1,), (1,)), ((), ())), preferred_element_type=f32
        ).astype(bf16)
        pieces = exchange(pieces.reshape(parts, groups, block), "tensor")
        normed_grad = jnp.sum(pieces.astype(f32), axis=0)
        x_s = x_blocks[section]
        inv = inverse[section]
        mean_term = lax.psum(jnp.sum(normed_grad * x_s, axis=-1, keepdims=True), "dp") / width
        grad_f = grad.astype(f32) + inv * normed_grad - x_s * inv**3 * mean_term
        grad = grad_f.astype(bf16)
        out_store.append(grad)

    grads = exchange(jnp.stack(rows_store[::-1]), "pipe").reshape(-1, block)
    pres = exchange(jnp.stack(pre_store[::-1]), "pipe")
    hidden_all = jnp.transpose(
        hidden_all.reshape(groups, parts, pipe, hidden_width), (2, 1, 0, 3)
    ).reshape(-1, hidden_width)
    down_grad = lax.dot_general(
        hidden_all, grads, (((0,), (0,)), ((), ())), preferred_element_type=f32
    ).astype(bf16)
    pres = jnp.transpose(
        pres.reshape(pipe, parts, groups, hidden_width), (1, 2, 0, 3)
    ).reshape(-1, hidden_width)
    up_grad = lax.dot_general(
        normed_all.reshape(-1, block), pres, (((0,), (0,)), ((), ())), preferred_element_type=f32
    ).astype(bf16)

    outs = exchange(jnp.stack(out_store[::-1]).reshape(pipe * groups, block), ("pipe", "dp"))
    input_grad = outs.reshape(1, 1, 1, own_rows, width)
    return (input_grad, up_grad[None], down_grad[None])


def solution(mesh):
    return jax.shard_map(
        per_device,
        mesh=mesh,
        in_specs=(
            P("pipe", None, "dp", "tensor", None),
            P("pipe", None, "dp", None, "tensor"),
            P(None, "dp", "tensor", None),
            P("pipe", "dp", "tensor"),
            P("pipe", "tensor", "dp"),
        ),
        out_specs=(
            P("pipe", None, "dp", "tensor", None),
            P("pipe", "dp", "tensor"),
            P("pipe", "tensor", "dp"),
        ),
        check_vma=False,
    )
```

```python
import jax
import jax.numpy as jnp
from jax import lax
from jax.sharding import PartitionSpec as P

epsilon = 1e-06
f32 = jnp.float32
bf16 = jnp.bfloat16
LANES = 128


def exchange(blocks, axis):
    shape = blocks.shape
    flat = blocks.reshape(shape[0], -1, LANES)
    return lax.all_to_all(flat, axis, 0, 0).reshape(shape)


def after(value, *others):
    return lax.optimization_barrier((value,) + others)[0]


def slope_of(u):
    sigmoid_u = jax.nn.sigmoid(u)
    return sigmoid_u * (1.0 + u * (1.0 - sigmoid_u))


def dot_nt(left, right):
    product = lax.dot_general(left, right, (((1,), (1,)), ((), ())), preferred_element_type=f32)
    return product.astype(bf16)


def dot_tn(left, right):
    product = lax.dot_general(left, right, (((0,), (0,)), ((), ())), preferred_element_type=f32)
    return product.astype(bf16)


def per_device(section_input, pre_act, cotangent, w_up, w_down):
    pipe = lax.axis_size("pipe")
    parts = lax.axis_size("tensor")
    groups = lax.axis_size("dp")
    pipe_index = lax.axis_index("pipe")
    own_rows, width = section_input.shape[-2:]
    block = width // groups
    rows, hidden_width = pre_act.shape[-2:]
    tokens = parts * groups

    x_own = section_input[0, 0, 0]
    u_own = pre_act[0, 0, 0]
    x_own_f = x_own.astype(f32)
    inverse_own = lax.rsqrt(jnp.mean(x_own_f * x_own_f, axis=-1, keepdims=True) + epsilon)
    normed_own = (x_own_f * inverse_own).astype(bf16)

    down_all = lax.all_gather(w_down[0], "pipe", axis=0)
    up_all = lax.all_gather(w_up[0], "pipe", axis=0)

    cot_blocks = exchange(jnp.swapaxes(cotangent[0, 0].reshape(own_rows, groups, block), 0, 1), "dp")
    cot_blocks = jnp.swapaxes(cot_blocks, 0, 1)
    normed_blocks = exchange(jnp.swapaxes(normed_own.reshape(own_rows, groups, block), 0, 1), "dp")
    normed_blocks = jnp.swapaxes(normed_blocks, 0, 1)

    x_blocks = exchange(x_own.reshape(pipe * groups, block), ("pipe", "dp"))
    x_blocks = x_blocks.reshape(pipe, groups, block).astype(f32)
    square = lax.psum(jnp.sum(x_blocks * x_blocks, axis=-1), "dp")
    inverse = lax.rsqrt(square / width + epsilon)[..., None]

    u_rows = jnp.swapaxes(u_own.reshape(parts, pipe, hidden_width), 0, 1)
    u_rows = exchange(u_rows, "pipe")
    u_rows = lax.all_gather(u_rows, "dp", axis=2)
    u_rows = u_rows.reshape(pipe, tokens, hidden_width).astype(f32)
    slope = slope_of(u_rows)

    u_f = u_own.astype(f32)
    slope_own = slope_of(u_f)
    hidden = (u_f * jax.nn.sigmoid(u_f)).astype(bf16)
    hidden_all = lax.all_gather(hidden, "dp", axis=0)
    hidden_all = hidden_all.reshape(groups, parts, pipe, hidden_width)

    last = pipe - 1
    is_last = pipe_index == last
    spread = jnp.broadcast_to(cot_blocks[None], (parts,) + cot_blocks.shape)
    cot_rows = exchange(spread, "tensor").reshape(-1, block)
    partial = dot_nt(cot_rows, w_down[0])
    partial = jnp.transpose(partial.reshape(parts, pipe, groups, hidden_width), (2, 0, 1, 3))
    hidden_grad = jnp.sum(exchange(partial, "dp").astype(f32), axis=0).reshape(rows, hidden_width)
    pre_last = lax.all_gather((hidden_grad * slope_own).astype(bf16), "dp", axis=0)
    pre_last = jnp.transpose(pre_last.reshape(groups, parts, pipe, hidden_width), (1, 2, 0, 3))
    pre_last = pre_last.reshape(-1, hidden_width)
    pieces = exchange(dot_nt(pre_last, w_up[0]).reshape(parts, pipe * groups, block), "tensor")
    sums = jnp.sum(pieces.astype(f32), axis=0).reshape(pipe, groups, block)
    normed_grad = exchange(sums, "pipe")[last]

    normed_blocks = after(normed_blocks, up_all, down_all)
    normed_all = lax.all_gather(normed_blocks.reshape(-1, block), "tensor", axis=0, tiled=True)

    def finish(section, grad, normed_grad):
        x_s = x_blocks[section]
        inv = inverse[section]
        mean_term = lax.psum(jnp.sum(normed_grad * x_s, axis=-1, keepdims=True), "dp") / width
        grad_f = grad.astype(f32) + inv * normed_grad - x_s * inv**3 * mean_term
        return grad_f.astype(bf16)

    grad = lax.dynamic_index_in_dim(cot_blocks, pipe_index, 0, keepdims=False)
    grad = finish(last, grad, normed_grad)
    out_store = [grad]
    rows_store = [jnp.zeros((tokens, block), bf16)]
    pre_store = [jnp.zeros((tokens, hidden_width), bf16)]
    for section in reversed(range(last)):
        if section == 0:
            grad, normed_all = lax.optimization_barrier((grad, normed_all))
        spread = jnp.broadcast_to(grad[None], (parts,) + grad.shape)
        grad_rows = exchange(spread, "tensor").reshape(tokens, block)
        rows_store.append(grad_rows)
        partials = lax.all_gather(dot_nt(grad_rows, down_all[section]), "dp", axis=0)
        hidden_grad = jnp.sum(partials.astype(f32), axis=0)
        pre_grad = (hidden_grad * slope[section]).astype(bf16)
        pre_store.append(pre_grad)
        pieces = dot_nt(pre_grad, up_all[section]).reshape(parts, groups, block)
        pieces = exchange(pieces, "tensor")
        grad = finish(section, grad, jnp.sum(pieces.astype(f32), axis=0))
        out_store.append(grad)

    grads = exchange(jnp.stack(rows_store[::-1]), "pipe").reshape(-1, block)
    grads = jnp.where(is_last, cot_rows, grads)
    hidden_all = jnp.where(
        is_last,
        jnp.transpose(hidden_all, (1, 2, 0, 3)).reshape(-1, hidden_width),
        jnp.transpose(hidden_all, (2, 1, 0, 3)).reshape(-1, hidden_width),
    )
    down_grad = dot_tn(hidden_all, grads)
    pres = exchange(jnp.stack(pre_store[::-1]), "pipe")
    pres = jnp.swapaxes(pres.reshape(pipe, parts, groups, hidden_width), 0, 1)
    pres = jnp.where(is_last, pre_last, pres.reshape(-1, hidden_width))
    up_grad = dot_tn(normed_all, pres)

    outs = exchange(jnp.stack(out_store[::-1]).reshape(pipe * groups, block), ("pipe", "dp"))
    input_grad = outs.reshape(1, 1, 1, own_rows, width)
    return (input_grad, up_grad[None], down_grad[None])


def solution(mesh):
    return jax.shard_map(
        per_device,
        mesh=mesh,
        in_specs=(
            P("pipe", None, "dp", "tensor", None),
            P("pipe", None, "dp", None, "tensor"),
            P(None, "dp", "tensor", None),
            P("pipe", "dp", "tensor"),
            P("pipe", "tensor", "dp"),
        ),
        out_specs=(
            P("pipe", None, "dp", "tensor", None),
            P("pipe", "dp", "tensor"),
            P("pipe", "tensor", "dp"),
        ),
        check_vma=False,
    )
```

```python
import jax
import jax.numpy as jnp
from jax import lax
from jax.sharding import PartitionSpec as P

epsilon = 1e-06
f32 = jnp.float32
bf16 = jnp.bfloat16
LANES = 128


def exchange(blocks, axis, count):
    flat = blocks.reshape(count, -1, LANES)
    return lax.all_to_all(flat, axis, 0, 0).reshape(blocks.shape)


def after(value, *others):
    return lax.optimization_barrier((value,) + others)[0]


def shifted(value, steps):
    count = lax.axis_size("pipe")
    return lax.ppermute(value, "pipe", [(i, (i + steps) % count) for i in range(count)])


def choose(index, options):
    result = options[-1]
    for k in reversed(range(len(options) - 1)):
        result = jnp.where(index == k, options[k], result)
    return result


def slope_of(u):
    sigmoid_u = jax.nn.sigmoid(u)
    return sigmoid_u * (1.0 + u * (1.0 - sigmoid_u))


def dot_nt(left, right):
    product = lax.dot_general(left, right, (((1,), (1,)), ((), ())), preferred_element_type=f32)
    return product.astype(bf16)


def dot_tn(left, right):
    product = lax.dot_general(left, right, (((0,), (0,)), ((), ())), preferred_element_type=f32)
    return product.astype(bf16)


def per_device(section_input, pre_act, cotangent, w_up, w_down):
    pipe = lax.axis_size("pipe")
    parts = lax.axis_size("tensor")
    groups = lax.axis_size("dp")
    pipe_index = lax.axis_index("pipe")
    own_rows, width = section_input.shape[-2:]
    block = width // groups
    rows, hidden_width = pre_act.shape[-2:]
    tokens = parts * groups

    x_own = section_input[0, 0, 0]
    u_own = pre_act[0, 0, 0]
    x_own_f = x_own.astype(f32)
    inverse_own = lax.rsqrt(jnp.mean(x_own_f * x_own_f, axis=-1, keepdims=True) + epsilon)
    normed_own = (x_own_f * inverse_own).astype(bf16)

    down_own, up_own = w_down[0], w_up[0]
    down_prev, up_next = shifted(down_own, 1), shifted(up_own, -1)
    down_next, up_prev = shifted(down_own, -1), shifted(up_own, 1)
    down_all = (down_own, down_next, shifted(down_prev, 1), down_prev)
    up_all = (up_own, up_next, shifted(up_next, -1), up_prev)

    inverse_high = inverse_own.astype(bf16)
    inverse_low = (inverse_own - inverse_high.astype(f32)).astype(bf16)
    lanes = jnp.concatenate(
        [inverse_high, inverse_low, jnp.zeros((own_rows, LANES - 2), bf16)], axis=-1
    )
    lanes = jnp.broadcast_to(lanes[:, None, None], (own_rows, groups, 1, LANES))
    u_spread = jnp.swapaxes(u_own.reshape(parts, pipe, hidden_width), 0, 1)
    u_spread = jnp.broadcast_to(
        u_spread.reshape(pipe, 1, -1, LANES), (pipe, groups, parts * hidden_width // LANES, LANES)
    )
    lines = block // LANES
    mixed = [
        x_own.reshape(own_rows, groups, lines, LANES),
        cotangent[0, 0].reshape(own_rows, groups, lines, LANES),
        u_spread,
        lanes,
    ]
    mixed = after(jnp.concatenate(mixed, 2), down_prev, up_next)
    mixed = exchange(mixed, ("pipe", "dp"), pipe * groups)
    mixed = mixed.reshape(pipe, groups, -1, LANES)
    x_blocks = mixed[:, :, :lines].reshape(pipe, groups, block).astype(f32)
    grad = mixed[0, :, lines : 2 * lines].reshape(groups, block)
    u_rows = jnp.swapaxes(mixed[:, :, 2 * lines : -1].reshape(pipe, groups, parts, hidden_width), 1, 2)
    slope = slope_of(u_rows.reshape(pipe, tokens, hidden_width).astype(f32))
    inverse = mixed[:, :, -1, :1].astype(f32) + mixed[:, :, -1, 1:2].astype(f32)

    normed_blocks = jnp.swapaxes(normed_own.reshape(own_rows, groups, block), 0, 1)
    normed_blocks = jnp.swapaxes(exchange(normed_blocks, "dp", groups), 0, 1).reshape(-1, block)
    normed_all = lax.all_gather(normed_blocks, "tensor", axis=0, tiled=True)

    u_f = u_own.astype(f32)
    hidden = lax.all_gather((u_f * jax.nn.sigmoid(u_f)).astype(bf16), "dp", axis=0)
    hidden = jnp.transpose(hidden.reshape(groups, parts, pipe, hidden_width), (2, 1, 0, 3))
    hidden = hidden.reshape(pipe, tokens, hidden_width)
    hidden = jnp.concatenate(
        [choose(pipe_index, [hidden[(p - k) % pipe] for p in range(pipe)]) for k in range(pipe)], 0
    )

    stores, out_store = [None] * pipe, [None] * pipe
    for section in reversed(range(pipe)):
        place = jnp.remainder(section - pipe_index, pipe)
        if section == 1:
            grad = after(grad, hidden)
        spread = jnp.broadcast_to(grad[None], (parts,) + grad.shape)
        grad_rows = exchange(spread, "tensor", parts).reshape(tokens, block)
        partials = lax.all_gather(dot_nt(grad_rows, choose(place, down_all)), "dp", axis=0)
        hidden_grad = jnp.sum(partials.astype(f32), axis=0)
        pre_grad = (hidden_grad * slope[section]).astype(bf16)
        stores[section] = jnp.concatenate([grad_rows, pre_grad], -1)
        pieces = dot_nt(pre_grad, choose(place, up_all)).reshape(parts, groups, block)
        pieces = exchange(pieces, "tensor", parts)
        if section == pipe - 1:
            pieces = after(pieces, normed_all)
        normed_grad = jnp.sum(pieces.astype(f32), axis=0)
        if section == 0:
            out_store[0] = normed_grad.astype(bf16)
            break
        x_s, inv = x_blocks[section], inverse[section]
        mean_term = lax.psum(jnp.sum(normed_grad * x_s, axis=-1, keepdims=True), "dp") / width
        grad_f = grad.astype(f32) + inv * normed_grad - x_s * inv**3 * mean_term
        grad = grad_f.astype(bf16)
        out_store[section] = grad

    outs = jnp.stack([jnp.stack(out_store), jnp.broadcast_to(grad, (pipe,) + grad.shape)], 2)
    outs = exchange(outs, ("pipe", "dp"), pipe * groups)
    outs = outs.reshape(own_rows, groups, 2, block)
    whole = outs[:, :, 0].reshape(own_rows, width)
    normed_grad = whole.astype(f32)
    above = outs[:, :, 1].reshape(own_rows, width).astype(f32)
    mean_term = jnp.mean(normed_grad * x_own_f, axis=-1, keepdims=True)
    grad_f = above + inverse_own * normed_grad - x_own_f * inverse_own**3 * mean_term
    input_grad = jnp.where(pipe_index == 0, grad_f.astype(bf16), whole)
    input_grad = input_grad.reshape(1, 1, 1, own_rows, width)

    moved = [choose(pipe_index, stores)]
    for k in range(1, pipe):
        chosen = choose(pipe_index, [stores[(p + k) % pipe] for p in range(pipe)])
        moved.append(shifted(chosen, k))
    moved = lax.optimization_barrier((moved, outs))[0]
    grads = jnp.concatenate([piece[:, :block] for piece in moved], 0)
    down_grad = dot_tn(hidden, grads)
    pres = [piece[:, block:] for piece in moved]
    pres = [choose(pipe_index, [pres[(p - i) % pipe] for p in range(pipe)]) for i in range(pipe)]
    pres = jnp.stack([piece.reshape(parts, groups, hidden_width) for piece in pres], 1)
    up_grad = dot_tn(normed_all, pres.reshape(-1, hidden_width))
    return (input_grad, up_grad[None], down_grad[None])


def solution(mesh):
    return jax.shard_map(
        per_device,
        mesh=mesh,
        in_specs=(
            P("pipe", None, "dp", "tensor", None),
            P("pipe", None, "dp", None, "tensor"),
            P(None, "dp", "tensor", None),
            P("pipe", "dp", "tensor"),
            P("pipe", "tensor", "dp"),
        ),
        out_specs=(
            P("pipe", None, "dp", "tensor", None),
            P("pipe", "dp", "tensor"),
            P("pipe", "tensor", "dp"),
        ),
        check_vma=False,
    )
```

```python
import jax
import jax.numpy as jnp
from jax import lax
from jax.sharding import PartitionSpec as P

epsilon = 1e-06
f32 = jnp.float32
bf16 = jnp.bfloat16
LANES = 128


def exchange(blocks, axis, count):
    flat = blocks if blocks.shape[0] == count else blocks.reshape(count, -1, LANES)
    return lax.all_to_all(flat, axis, 0, 0).reshape(blocks.shape)


def after(value, *others):
    return lax.optimization_barrier((value,) + others)[0]


def shifted(value, steps):
    count = lax.axis_size("pipe")
    return lax.ppermute(value, "pipe", [(i, (i + steps) % count) for i in range(count)])


def choose(index, options):
    result = options[-1]
    for k in reversed(range(len(options) - 1)):
        result = jnp.where(index == k, options[k], result)
    return result


def slope_of(u):
    sigmoid_u = jax.nn.sigmoid(u)
    return sigmoid_u * (1.0 + u * (1.0 - sigmoid_u))


def dot_nt(left, right):
    product = lax.dot_general(left, right, (((1,), (1,)), ((), ())), preferred_element_type=f32)
    return product.astype(bf16)


def dot_tn(left, right):
    product = lax.dot_general(left, right, (((0,), (0,)), ((), ())), preferred_element_type=f32)
    return product.astype(bf16)


def per_device(section_input, pre_act, cotangent, w_up, w_down):
    pipe = lax.axis_size("pipe")
    parts = lax.axis_size("tensor")
    groups = lax.axis_size("dp")
    pipe_index = lax.axis_index("pipe")
    own_rows, width = section_input.shape[-2:]
    block = width // groups
    rows, hidden_width = pre_act.shape[-2:]
    tokens = parts * groups

    x_own = section_input[0, 0, 0]
    u_own = pre_act[0, 0, 0]
    x_own_f = x_own.astype(f32)
    inverse_own = lax.rsqrt(jnp.mean(x_own_f * x_own_f, axis=-1, keepdims=True) + epsilon)
    normed_own = (x_own_f * inverse_own).astype(bf16)

    down_own, up_own = w_down[0], w_up[0]
    down_prev, up_next = shifted(down_own, 1), shifted(up_own, -1)
    down_next, up_prev = shifted(down_own, -1), shifted(up_own, 1)
    down_all = (down_own, down_next, shifted(down_prev, 1), down_prev)
    up_all = (up_own, up_next, shifted(up_next, -1), up_prev)

    inverse_high = inverse_own.astype(bf16)
    inverse_low = (inverse_own - inverse_high.astype(f32)).astype(bf16)
    lanes = jnp.concatenate(
        [inverse_high, inverse_low, jnp.zeros((own_rows, LANES - 2), bf16)], axis=-1
    )
    lanes = jnp.broadcast_to(lanes[:, None, None], (own_rows, groups, 1, LANES))
    u_spread = jnp.swapaxes(u_own.reshape(parts, pipe, hidden_width), 0, 1)
    u_spread = jnp.broadcast_to(
        u_spread.reshape(pipe, 1, -1, LANES), (pipe, groups, parts * hidden_width // LANES, LANES)
    )
    lines = block // LANES
    mixed = [
        x_own.reshape(own_rows, groups, lines, LANES),
        cotangent[0, 0].reshape(own_rows, groups, lines, LANES),
        u_spread,
        lanes,
    ]
    mixed = after(jnp.concatenate(mixed, 2), down_prev, up_next)
    mixed = exchange(mixed, ("pipe", "dp"), pipe * groups)
    mixed = mixed.reshape(pipe, groups, -1, LANES)
    x_blocks = mixed[:, :, :lines].reshape(pipe, groups, block).astype(f32)
    grad = mixed[0, :, lines : 2 * lines].reshape(groups, block)
    u_rows = jnp.swapaxes(mixed[:, :, 2 * lines : -1].reshape(pipe, groups, parts, hidden_width), 1, 2)
    slope = slope_of(u_rows.reshape(pipe, tokens, hidden_width).astype(f32))
    inverse = mixed[:, :, -1, :1].astype(f32) + mixed[:, :, -1, 1:2].astype(f32)

    normed_blocks = jnp.swapaxes(normed_own.reshape(own_rows, groups, block), 0, 1)
    normed_blocks = jnp.swapaxes(exchange(normed_blocks, "dp", groups), 0, 1).reshape(-1, block)
    normed_all = lax.all_gather(normed_blocks, "tensor", axis=0, tiled=True)

    u_f = u_own.astype(f32)
    hidden = lax.all_gather((u_f * jax.nn.sigmoid(u_f)).astype(bf16), "dp", axis=0)
    hidden = jnp.transpose(hidden.reshape(groups, parts, pipe, hidden_width), (2, 1, 0, 3))
    hidden = hidden.reshape(pipe, tokens, hidden_width)
    hidden = jnp.concatenate(
        [choose(pipe_index, [hidden[(p - k) % pipe] for p in range(pipe)]) for k in range(pipe)], 0
    )

    stores, out_store = [None] * pipe, [None] * pipe
    for section in reversed(range(pipe)):
        place = jnp.remainder(section - pipe_index, pipe)
        if section == 1:
            grad = after(grad, hidden)
        spread = jnp.broadcast_to(grad[None], (parts,) + grad.shape)
        grad_rows = exchange(spread, "tensor", parts).reshape(tokens, block)
        partials = lax.all_gather(dot_nt(grad_rows, choose(place, down_all)), "dp", axis=0)
        hidden_grad = jnp.sum(partials.astype(f32), axis=0)
        pre_grad = (hidden_grad * slope[section]).astype(bf16)
        stores[section] = jnp.concatenate([grad_rows, pre_grad], -1)
        pieces = dot_nt(pre_grad, choose(place, up_all)).reshape(parts, groups, block)
        pieces = exchange(pieces, "tensor", parts)
        if section == pipe - 1:
            pieces = after(pieces, normed_all)
        normed_grad = jnp.sum(pieces.astype(f32), axis=0)
        if section == 0:
            out_store[0] = normed_grad.astype(bf16)
            break
        x_s, inv = x_blocks[section], inverse[section]
        mean_term = lax.psum(jnp.sum(normed_grad * x_s, axis=-1, keepdims=True), "dp") / width
        grad_f = grad.astype(f32) + inv * normed_grad - x_s * inv**3 * mean_term
        grad = grad_f.astype(bf16)
        out_store[section] = grad

    outs = jnp.stack([jnp.stack(out_store), jnp.broadcast_to(grad, (pipe,) + grad.shape)], 2)
    outs = exchange(outs, ("pipe", "dp"), pipe * groups)
    outs = outs.reshape(own_rows, groups, 2, block)
    whole = outs[:, :, 0].reshape(own_rows, width)
    normed_grad = whole.astype(f32)
    above = outs[:, :, 1].reshape(own_rows, width).astype(f32)
    mean_term = jnp.mean(normed_grad * x_own_f, axis=-1, keepdims=True)
    grad_f = above + inverse_own * normed_grad - x_own_f * inverse_own**3 * mean_term
    input_grad = jnp.where(pipe_index == 0, grad_f.astype(bf16), whole)
    input_grad = input_grad.reshape(1, 1, 1, own_rows, width)

    moved = [choose(pipe_index, stores)]
    for k in range(1, pipe):
        chosen = choose(pipe_index, [stores[(p + k) % pipe] for p in range(pipe)])
        moved.append(shifted(chosen, k))
    moved = lax.optimization_barrier((moved, outs))[0]
    down_grad = dot_tn(hidden, jnp.concatenate(moved, 0))[:, :block]
    pres = [piece[:, block:] for piece in moved]
    pres = [choose(pipe_index, [pres[(p - i) % pipe] for p in range(pipe)]) for i in range(pipe)]
    pres = jnp.stack([piece.reshape(parts, groups, hidden_width) for piece in pres], 1)
    up_grad = dot_tn(normed_all, pres.reshape(-1, hidden_width))
    return (input_grad, up_grad[None], down_grad[None])


def solution(mesh):
    return jax.shard_map(
        per_device,
        mesh=mesh,
        in_specs=(
            P("pipe", None, "dp", "tensor", None),
            P("pipe", None, "dp", None, "tensor"),
            P(None, "dp", "tensor", None),
            P("pipe", "dp", "tensor"),
            P("pipe", "tensor", "dp"),
        ),
        out_specs=(
            P("pipe", None, "dp", "tensor", None),
            P("pipe", "dp", "tensor"),
            P("pipe", "tensor", "dp"),
        ),
        check_vma=False,
    )
```

```python
import jax
import jax.numpy as jnp
from jax import lax
from jax.sharding import PartitionSpec as P

epsilon = 1e-06
f32 = jnp.float32
bf16 = jnp.bfloat16
LANES = 128


def exchange(blocks, axis, count):
    flat = blocks if blocks.shape[0] == count else blocks.reshape(count, -1, LANES)
    return lax.all_to_all(flat, axis, 0, 0).reshape(blocks.shape)


def after(value, *others):
    return lax.optimization_barrier((value,) + others)[0]


def shifted(value, steps):
    count = lax.axis_size("pipe")
    return lax.ppermute(value, "pipe", [(i, (i + steps) % count) for i in range(count)])


def across(stores, section):
    source = (section + 2) % len(stores)
    return lax.ppermute(stores[section], "pipe", [(source, section)])


def choose(index, options):
    result = options[-1]
    for k in reversed(range(len(options) - 1)):
        result = jnp.where(index == k, options[k], result)
    return result


def slope_of(u):
    sigmoid_u = jax.nn.sigmoid(u)
    return sigmoid_u * (1.0 + u * (1.0 - sigmoid_u))


def dot_nt(left, right):
    product = lax.dot_general(left, right, (((1,), (1,)), ((), ())), preferred_element_type=f32)
    return product.astype(bf16)


def dot_tn(left, right):
    product = lax.dot_general(left, right, (((0,), (0,)), ((), ())), preferred_element_type=f32)
    return product.astype(bf16)


def per_device(section_input, pre_act, cotangent, w_up, w_down):
    pipe = lax.axis_size("pipe")
    parts = lax.axis_size("tensor")
    groups = lax.axis_size("dp")
    pipe_index = lax.axis_index("pipe")
    own_rows, width = section_input.shape[-2:]
    block = width // groups
    rows, hidden_width = pre_act.shape[-2:]
    tokens = parts * groups

    x_own = section_input[0, 0, 0]
    u_own = pre_act[0, 0, 0]
    x_own_f = x_own.astype(f32)
    inverse_own = lax.rsqrt(jnp.mean(x_own_f * x_own_f, axis=-1, keepdims=True) + epsilon)
    normed_own = (x_own_f * inverse_own).astype(bf16)

    down_own, up_own = w_down[0], w_up[0]
    down_prev, up_next = shifted(down_own, 1), shifted(up_own, -1)
    down_next, up_prev = shifted(down_own, -1), shifted(up_own, 1)
    down_all = (down_own, down_next, shifted(down_prev, 1), down_prev)
    up_all = (up_own, up_next, shifted(up_next, -1), up_prev)

    inverse_high = inverse_own.astype(bf16)
    inverse_low = (inverse_own - inverse_high.astype(f32)).astype(bf16)
    lanes = jnp.concatenate(
        [inverse_high, inverse_low, jnp.zeros((own_rows, LANES - 2), bf16)], axis=-1
    )
    lanes = jnp.broadcast_to(lanes[:, None, None], (own_rows, groups, 1, LANES))
    u_spread = jnp.swapaxes(u_own.reshape(parts, pipe, hidden_width), 0, 1)
    u_spread = jnp.broadcast_to(
        u_spread.reshape(pipe, 1, -1, LANES), (pipe, groups, parts * hidden_width // LANES, LANES)
    )
    lines = block // LANES
    mixed = [
        x_own.reshape(own_rows, groups, lines, LANES),
        cotangent[0, 0].reshape(own_rows, groups, lines, LANES),
        u_spread,
        lanes,
    ]
    mixed = after(jnp.concatenate(mixed, 2), down_prev, up_next)
    mixed = exchange(mixed, ("pipe", "dp"), pipe * groups)
    mixed = mixed.reshape(pipe, groups, -1, LANES)
    x_blocks = mixed[:, :, :lines].reshape(pipe, groups, block).astype(f32)
    grad = mixed[0, :, lines : 2 * lines].reshape(groups, block)
    u_rows = jnp.swapaxes(mixed[:, :, 2 * lines : -1].reshape(pipe, groups, parts, hidden_width), 1, 2)
    slope = slope_of(u_rows.reshape(pipe, tokens, hidden_width).astype(f32))
    inverse = mixed[:, :, -1, :1].astype(f32) + mixed[:, :, -1, 1:2].astype(f32)

    normed_blocks = jnp.swapaxes(normed_own.reshape(own_rows, groups, block), 0, 1)
    normed_blocks = jnp.swapaxes(exchange(normed_blocks, "dp", groups), 0, 1).reshape(-1, block)
    normed_all = lax.all_gather(normed_blocks, "tensor", axis=0, tiled=True)

    stores, out_store, opposite = [None] * pipe, [None] * pipe, []
    for section in reversed(range(pipe)):
        place = jnp.remainder(section - pipe_index, pipe)
        if section == pipe - 2:
            grad, u_late = lax.optimization_barrier((grad, u_own))
            u_late = u_late.astype(f32)
            hidden_own = (u_late * jax.nn.sigmoid(u_late)).astype(bf16)
            hidden = lax.all_gather(hidden_own, "dp", axis=0)
        spread = jnp.broadcast_to(grad[None], (parts,) + grad.shape)
        grad_rows = exchange(spread, "tensor", parts).reshape(tokens, block)
        if section < pipe - 2:
            far = across(stores, 3 if section == 1 else 1)
            opposite.append(far)
            grad_rows = after(grad_rows, far)
        partials = lax.all_gather(dot_nt(grad_rows, choose(place, down_all)), "dp", axis=0)
        hidden_grad = jnp.sum(partials.astype(f32), axis=0)
        pre_grad = (hidden_grad * slope[section]).astype(bf16)
        stores[section] = jnp.concatenate([grad_rows, pre_grad], -1)
        pieces = dot_nt(pre_grad, choose(place, up_all)).reshape(parts, groups, block)
        pieces = exchange(pieces, "tensor", parts)
        if section == pipe - 2:
            pieces, hidden = lax.optimization_barrier((pieces, hidden))
        if section == 1:
            far = across(stores, 2)
            opposite.append(far)
            pieces = after(pieces, far)
        if section == pipe - 1:
            pieces = after(pieces, normed_all)
        normed_grad = jnp.sum(pieces.astype(f32), axis=0)
        if section == 0:
            out_store[0] = normed_grad.astype(bf16)
            break
        x_s, inv = x_blocks[section], inverse[section]
        mean_term = lax.psum(jnp.sum(normed_grad * x_s, axis=-1, keepdims=True), "dp") / width
        grad_f = grad.astype(f32) + inv * normed_grad - x_s * inv**3 * mean_term
        grad = grad_f.astype(bf16)
        out_store[section] = grad

    outs = jnp.stack([jnp.stack(out_store), jnp.broadcast_to(grad, (pipe,) + grad.shape)], 2)
    outs = exchange(outs, ("pipe", "dp"), pipe * groups)
    outs = outs.reshape(own_rows, groups, 2, block)
    whole = outs[:, :, 0].reshape(own_rows, width)
    normed_grad = whole.astype(f32)
    above = outs[:, :, 1].reshape(own_rows, width).astype(f32)
    mean_term = jnp.mean(normed_grad * x_own_f, axis=-1, keepdims=True)
    grad_f = above + inverse_own * normed_grad - x_own_f * inverse_own**3 * mean_term
    input_grad = jnp.where(pipe_index == 0, grad_f.astype(bf16), whole)
    input_grad = input_grad.reshape(1, 1, 1, own_rows, width)

    moved = [choose(pipe_index, stores)]
    for k in (1, 3):
        chosen = choose(pipe_index, [stores[(p + k) % pipe] for p in range(pipe)])
        moved.append(shifted(chosen, k))
    third, second, first = opposite
    moved.insert(2, choose(pipe_index, [across(stores, 0), first, second, third]))
    moved = lax.optimization_barrier((moved, outs))[0]
    hidden = jnp.transpose(hidden.reshape(groups, parts, pipe, hidden_width), (2, 1, 0, 3))
    hidden = hidden.reshape(pipe, tokens, hidden_width)
    hidden = jnp.concatenate(
        [choose(pipe_index, [hidden[(p - k) % pipe] for p in range(pipe)]) for k in range(pipe)], 0
    )
    down_grad = dot_tn(hidden, jnp.concatenate(moved, 0))[:, :block]
    pres = [piece[:, block:] for piece in moved]
    pres = [choose(pipe_index, [pres[(p - i) % pipe] for p in range(pipe)]) for i in range(pipe)]
    pres = jnp.stack([piece.reshape(parts, groups, hidden_width) for piece in pres], 1)
    up_grad = dot_tn(normed_all, pres.reshape(-1, hidden_width))
    return (input_grad, up_grad[None], down_grad[None])


def solution(mesh):
    return jax.shard_map(
        per_device,
        mesh=mesh,
        in_specs=(
            P("pipe", None, "dp", "tensor", None),
            P("pipe", None, "dp", None, "tensor"),
            P(None, "dp", "tensor", None),
            P("pipe", "dp", "tensor"),
            P("pipe", "tensor", "dp"),
        ),
        out_specs=(
            P("pipe", None, "dp", "tensor", None),
            P("pipe", "dp", "tensor"),
            P("pipe", "tensor", "dp"),
        ),
        check_vma=False,
    )
```

```python
import jax
import jax.numpy as jnp
from jax import lax
from jax.sharding import PartitionSpec as P

epsilon = 1e-06
f32 = jnp.float32
bf16 = jnp.bfloat16
LANES = 128


def exchange(blocks, axis, count):
    flat = blocks if blocks.shape[0] == count else blocks.reshape(count, -1, LANES)
    return lax.all_to_all(flat, axis, 0, 0).reshape(blocks.shape)


def after(value, *others):
    return lax.optimization_barrier((value,) + others)[0]


def shifted(value, steps):
    count = lax.axis_size("pipe")
    return lax.ppermute(value, "pipe", [(i, (i + steps) % count) for i in range(count)])


def across(stores, section):
    source = (section + 2) % len(stores)
    return lax.ppermute(stores[section], "pipe", [(source, section)])


def choose(index, options):
    result = options[-1]
    for k in reversed(range(len(options) - 1)):
        result = jnp.where(index == k, options[k], result)
    return result


def slope_of(u):
    sigmoid_u = jax.nn.sigmoid(u)
    return sigmoid_u * (1.0 + u * (1.0 - sigmoid_u))


def dot_nt(left, right):
    product = lax.dot_general(left, right, (((1,), (1,)), ((), ())), preferred_element_type=f32)
    return product.astype(bf16)


def dot_tn(left, right):
    product = lax.dot_general(left, right, (((0,), (0,)), ((), ())), preferred_element_type=f32)
    return product.astype(bf16)


def per_device(section_input, pre_act, cotangent, w_up, w_down):
    pipe = lax.axis_size("pipe")
    parts = lax.axis_size("tensor")
    groups = lax.axis_size("dp")
    pipe_index = lax.axis_index("pipe")
    own_rows, width = section_input.shape[-2:]
    block = width // groups
    rows, hidden_width = pre_act.shape[-2:]
    tokens = parts * groups

    x_own = section_input[0, 0, 0]
    u_own = pre_act[0, 0, 0]
    x_own_f = x_own.astype(f32)
    inverse_own = lax.rsqrt(jnp.mean(x_own_f * x_own_f, axis=-1, keepdims=True) + epsilon)
    normed_own = (x_own_f * inverse_own).astype(bf16)

    down_own, up_own = w_down[0], w_up[0]
    down_prev, up_next = shifted(down_own, 1), shifted(up_own, -1)
    down_next, up_prev = shifted(down_own, -1), shifted(up_own, 1)
    down_all = (down_own, down_next, shifted(down_prev, 1), down_prev)
    up_all = (up_own, up_next, shifted(up_next, -1), up_prev)

    inverse_high = inverse_own.astype(bf16)
    inverse_low = (inverse_own - inverse_high.astype(f32)).astype(bf16)
    lanes = jnp.concatenate(
        [inverse_high, inverse_low, jnp.zeros((own_rows, LANES - 2), bf16)], axis=-1
    )
    lanes = jnp.broadcast_to(lanes[:, None, None], (own_rows, groups, 1, LANES))
    u_spread = jnp.swapaxes(u_own.reshape(parts, pipe, hidden_width), 0, 1)
    u_spread = jnp.broadcast_to(
        u_spread.reshape(pipe, 1, -1, LANES), (pipe, groups, parts * hidden_width // LANES, LANES)
    )
    lines = block // LANES
    mixed = [
        x_own.reshape(own_rows, groups, lines, LANES),
        cotangent[0, 0].reshape(own_rows, groups, lines, LANES),
        u_spread,
        lanes,
    ]
    mixed = after(jnp.concatenate(mixed, 2), down_prev, up_next)
    mixed = exchange(mixed, ("pipe", "dp"), pipe * groups)
    mixed = mixed.reshape(pipe, groups, -1, LANES)
    x_blocks = mixed[:, :, :lines].reshape(pipe, groups, block).astype(f32)
    grad = mixed[0, :, lines : 2 * lines].reshape(groups, block)
    u_rows = jnp.swapaxes(mixed[:, :, 2 * lines : -1].reshape(pipe, groups, parts, hidden_width), 1, 2)
    slope = slope_of(u_rows.reshape(pipe, tokens, hidden_width).astype(f32))
    inverse = mixed[:, :, -1, :1].astype(f32) + mixed[:, :, -1, 1:2].astype(f32)

    normed_blocks = jnp.swapaxes(normed_own.reshape(own_rows, groups, block), 0, 1)
    normed_blocks = jnp.swapaxes(exchange(normed_blocks, "dp", groups), 0, 1).reshape(-1, block)
    normed_all = lax.all_gather(normed_blocks, "tensor", axis=0, tiled=True)

    stores, out_store, opposite = [None] * pipe, [None] * pipe, []
    for section in reversed(range(pipe)):
        place = jnp.remainder(section - pipe_index, pipe)
        if section == pipe - 2:
            grad, u_late = lax.optimization_barrier((grad, u_own))
            u_late = u_late.astype(f32)
            hidden_own = (u_late * jax.nn.sigmoid(u_late)).astype(bf16)
            hidden = lax.all_gather(hidden_own, "dp", axis=0)
        spread = jnp.broadcast_to(grad[None], (parts,) + grad.shape)
        grad_rows = exchange(spread, "tensor", parts).reshape(tokens, block)
        if section < pipe - 2:
            far = across(stores, 3 if section == 1 else 1)
            opposite.append(far)
            grad_rows = after(grad_rows, far)
        partials = lax.all_gather(dot_nt(grad_rows, choose(place, down_all)), "dp", axis=0)
        hidden_grad = jnp.sum(partials.astype(f32), axis=0)
        pre_grad = (hidden_grad * slope[section]).astype(bf16)
        stores[section] = jnp.concatenate([grad_rows, pre_grad], -1)
        pieces = dot_nt(pre_grad, choose(place, up_all)).reshape(parts, groups, block)
        pieces = exchange(pieces, "tensor", parts)
        if section == pipe - 2:
            pieces, hidden = lax.optimization_barrier((pieces, hidden))
        if section == 1:
            far = across(stores, 2)
            opposite.append(far)
            pieces = after(pieces, far)
        if section == pipe - 1:
            pieces = after(pieces, normed_all)
        normed_grad = jnp.sum(pieces.astype(f32), axis=0)
        if section == 0:
            out_store[0] = normed_grad.astype(bf16)
            break
        x_s, inv = x_blocks[section], inverse[section]
        mean_term = lax.psum(jnp.sum(normed_grad * x_s, axis=-1, keepdims=True), "dp") / width
        grad_f = grad.astype(f32) + inv * normed_grad - x_s * inv**3 * mean_term
        grad = grad_f.astype(bf16)
        out_store[section] = grad

    outs = jnp.stack([jnp.stack(out_store), jnp.broadcast_to(grad, (pipe,) + grad.shape)], 2)
    unsent = outs
    outs = exchange(outs, ("pipe", "dp"), pipe * groups)
    outs = outs.reshape(own_rows, groups, 2, block)
    whole = outs[:, :, 0].reshape(own_rows, width)
    normed_grad = whole.astype(f32)
    above = outs[:, :, 1].reshape(own_rows, width).astype(f32)
    mean_term = jnp.mean(normed_grad * x_own_f, axis=-1, keepdims=True)
    grad_f = above + inverse_own * normed_grad - x_own_f * inverse_own**3 * mean_term
    input_grad = jnp.where(pipe_index == 0, grad_f.astype(bf16), whole)
    input_grad = input_grad.reshape(1, 1, 1, own_rows, width)

    moved = [choose(pipe_index, stores)]
    for k in (1, 3):
        chosen = choose(pipe_index, [stores[(p + k) % pipe] for p in range(pipe)])
        moved.append(shifted(chosen, k))
    third, second, first = opposite
    moved.insert(2, choose(pipe_index, [across(stores, 0), first, second, third]))
    moved = lax.optimization_barrier((moved, unsent))[0]
    hidden = jnp.transpose(hidden.reshape(groups, parts, pipe, hidden_width), (2, 1, 0, 3))
    hidden = hidden.reshape(pipe, tokens, hidden_width)
    hidden = jnp.concatenate(
        [choose(pipe_index, [hidden[(p - k) % pipe] for p in range(pipe)]) for k in range(pipe)], 0
    )
    down_grad = dot_tn(hidden, jnp.concatenate(moved, 0))[:, :block]
    pres = [piece[:, block:] for piece in moved]
    pres = [choose(pipe_index, [pres[(p - i) % pipe] for p in range(pipe)]) for i in range(pipe)]
    pres = jnp.stack([piece.reshape(parts, groups, hidden_width) for piece in pres], 1)
    up_grad = dot_tn(normed_all, pres.reshape(-1, hidden_width))
    return (input_grad, up_grad[None], down_grad[None])


def solution(mesh):
    return jax.shard_map(
        per_device,
        mesh=mesh,
        in_specs=(
            P("pipe", None, "dp", "tensor", None),
            P("pipe", None, "dp", None, "tensor"),
            P(None, "dp", "tensor", None),
            P("pipe", "dp", "tensor"),
            P("pipe", "tensor", "dp"),
        ),
        out_specs=(
            P("pipe", None, "dp", "tensor", None),
            P("pipe", "dp", "tensor"),
            P("pipe", "tensor", "dp"),
        ),
        check_vma=False,
    )
```
